128 devices in a mesh: row: 16 (over z_lo, y, core), col: 8 (over z_hi, x).
Axes of the slice: x: 4, y: 4, z: 4 (z_hi: 2, z_lo: 2; z = z_hi * 2 + z_lo), core: 2. Of those that a mesh axis runs over, the one named last changes fastest.
Arguments:
- coords: float32 [16, 65536], P(None, ('row', 'col')), may hold values from -6 to 6
- lengthscale: float32 [16], replicated, may hold values from 1.5 to 3
- solution: float32 [64, 65536], P(None, ('row', 'col')), may hold values from -6 to 6
- residual: float32 [64, 65536], P(None, ('row', 'col')), may hold values from -6 to 6
- direction: float32 [64, 65536], P(None, ('row', 'col')), may hold values from -6 to 6
Outputs:
- new_solution: float32 [64, 65536], P(None, ('row', 'col'))
- new_residual: float32 [64, 65536], P(None, ('row', 'col'))
- new_direction: float32 [64, 65536], P(None, ('row', 'col'))
The draws below stay inside these ranges and needn't reach their ends.
All inputs are finite; a program needn't handle non-finite values.
Results may differ from the reference program's by a relative error of at most 0.0054.
Values may be sent and summed in bfloat16 or wider, within the bound.
A program may use at most 64 MiB of HBM per device.

```python
import math
import jax
import jax.numpy as jnp
from jax import lax

FEATS = 16
PROBES = 64
NPTS = 65536


def block_scale(stream_key, shape, shards, smallest, high):
    factor_of = 1.0
    for dim, shards_of in shards:
        draws = jax.random.uniform(jax.random.fold_in(jax.random.fold_in(stream_key, 6), dim), (shards_of,), jnp.float32, smallest / len(shards), high / len(shards))
        factor_of = factor_of * jnp.repeat(jnp.exp(draws), shape[dim] // shards_of).reshape((-1,) + (1,) * (len(shape) - 1 - dim))
    return factor_of


def gaussian(own_key, dims, deviation, limit, pieces=(), dtype=jnp.bfloat16):
    level = block_scale(own_key, dims, pieces, -0.22, 0.18) if pieces else 1.0
    entries = jax.random.normal(own_key, dims, jnp.float32) * deviation * level
    return jnp.minimum(jnp.maximum(entries, -limit), limit).astype(dtype)


def setup_inputs(seed: int = 0) -> dict:
    key_list = jax.random.split(jax.random.key(seed), 6)
    coords = gaussian(key_list[0], (FEATS, NPTS), 1.0, 6.0, ((1, 128),), jnp.float32)
    lengthscale = jnp.clip(jnp.exp(jax.random.uniform(key_list[1], (FEATS,), jnp.float32, math.log(1.5), math.log(3.0))), 1.5, 3.0)
    solution = gaussian(key_list[2], (PROBES, NPTS), 1.0, 6.0, ((1, 128),), jnp.float32)
    residual = gaussian(key_list[3], (PROBES, NPTS), 1.0, 6.0, ((1, 128),), jnp.float32)
    direction = gaussian(key_list[4], (PROBES, NPTS), 1.0, 6.0, ((1, 128),), jnp.float32)
    return dict(coords=coords, lengthscale=lengthscale, solution=solution, residual=residual, direction=direction)


def matern(col_scaled, row_scaled, row_sq):
    col_sq = lax.optimization_barrier(jnp.sum(col_scaled.astype(jnp.float32) ** 2, axis=0))
    cross = lax.dot_general(col_scaled, row_scaled, (((0,), (0,)), ((), ())), preferred_element_type=jnp.float32)
    dist2 = jnp.maximum(col_sq[:, None] + row_sq[None, :] - 2.0 * cross, 0.0)
    radius = jnp.sqrt(dist2)
    root_five = math.sqrt(5.0)
    value = (1.0 + root_five * radius + 5.0 / 3.0 * dist2) * jnp.exp(-root_five * radius)
    return value.astype(jnp.bfloat16)

def reference(coords, lengthscale, solution, residual, direction):
    scaled = (coords / lengthscale[:, None]).astype(jnp.bfloat16)
    sqnorm = lax.optimization_barrier(jnp.sum(scaled.astype(jnp.float32) ** 2, axis=0))
    dir_half = direction.astype(jnp.bfloat16)
    total = NPTS
    width = math.gcd(total, 1024)
    nblocks = total // width
    row_blocks = scaled.reshape(FEATS, nblocks, width).transpose(1, 0, 2)
    sq_blocks = sqnorm.reshape(nblocks, width)

    def one_block(pair):
        kern = matern(scaled, pair[0], pair[1])
        return jnp.dot(dir_half, kern, preferred_element_type=jnp.float32)
    blocks = lax.map(one_block, (row_blocks, sq_blocks))
    image = blocks.transpose(1, 0, 2).reshape(PROBES, total) + direction
    norm_old = lax.optimization_barrier(jnp.sum(residual * residual, axis=1))
    curv = lax.optimization_barrier(jnp.sum(direction * image, axis=1))
    alpha = norm_old / curv
    new_solution = solution + alpha[:, None] * direction
    new_residual = residual - alpha[:, None] * image
    fresh = lax.optimization_barrier(jnp.sum(new_residual * new_residual, axis=1))
    new_direction = new_residual + (fresh / norm_old)[:, None] * direction
    return (new_solution, new_residual, new_direction)
```

```python
import math

import jax
import jax.numpy as jnp
from jax import lax
from jax.experimental import pallas as pl
from jax.experimental.pallas import tpu as pltpu
from jax.sharding import PartitionSpec as P

MESH = pl.DeviceIdType.MESH
F32 = jnp.float32
BF16 = jnp.bfloat16

NS = 8
NT = 8
NDEV = 128
HALF = 4
FEAT = 32
LN2 = math.log(2.0)
SCALE = 5.0 / LN2**2
SHIFT = 1.5 / LN2
CONST = 0.75 / LN2**2
FACTOR = LN2**2 / 3.0 * 2.0**SHIFT
WIDTH = 256


def entries(x):
    t = jnp.maximum(x, 1e-12)
    w = -SHIFT - t * lax.rsqrt(t)
    return ((w * w + CONST) * jnp.exp2(w)).astype(BF16)


def pieces(value):
    high = value.astype(BF16).astype(F32)
    mid = (value - high).astype(BF16).astype(F32)
    low = (value - high - mid).astype(BF16).astype(F32)
    return high, mid, low


def kernel(
    coords, scale, solution, residual, direction, new_solution, new_residual, new_direction,
    blk, left, right, dir_s, acc_s, acc_t, out, got, x0, x1, k0, k1, mine, part, one, two,
    blk_send, blk_recv, out_send, out_recv, one_send, one_recv, two_send, two_recv,
):
    ncol = NS
    me = lax.axis_index("row") * ncol + lax.axis_index("col")

    def device(offset):
        label = lax.rem(me + offset + NDEV, NDEV)
        return (label // ncol, lax.rem(label, ncol))

    def block_copy(slot, offset):
        return pltpu.make_async_remote_copy(
            src_ref=blk.at[0], dst_ref=blk.at[slot], send_sem=blk_send.at[slot], recv_sem=blk_recv.at[slot],
            device_id=device(offset), device_id_type=MESH,
        )

    def s_copy(s):
        return block_copy(s, -s)

    def t_copy(t):
        return block_copy(NS - 1 + t, -8 * t)

    def out_copy(slot, offset):
        return pltpu.make_async_remote_copy(
            src_ref=out.at[slot], dst_ref=got.at[slot], send_sem=out_send.at[slot], recv_sem=out_recv.at[slot],
            device_id=device(offset), device_id_type=MESH,
        )

    barrier = pltpu.get_barrier_semaphore()
    for s in range(1, NS):
        pl.semaphore_signal(barrier, inc=1, device_id=device(s), device_id_type=MESH)
        pl.semaphore_signal(barrier, inc=1, device_id=device(-s), device_id_type=MESH)
    for t in range(1, 16):
        pl.semaphore_signal(barrier, inc=1, device_id=device(8 * t), device_id_type=MESH)

    scaled = (coords[...] / scale[...]).astype(BF16)
    wide = scaled.astype(F32)
    sq = jnp.sum(wide * wide, axis=0, keepdims=True)
    high, mid, low = pieces(sq)
    rows = lax.broadcasted_iota(jnp.int32, (16, sq.shape[1]), 0)
    extra = jnp.where(rows == 0, high, jnp.where(rows == 1, mid, jnp.where(rows == 2, low, 0.0)))
    extra = jnp.where((rows >= 8) & (rows < 11), 1.0, extra)
    blk[0, 0:16, :] = scaled
    blk[0, 16:32, :] = extra.astype(BF16)
    blk[0, 32:96, :] = direction[...].astype(BF16)

    pl.semaphore_wait(barrier, 29)
    t_copy(1).start()
    for s in range(1, HALF):
        s_copy(s).start()
    for t in range(2, 5):
        t_copy(t).start()
    for s in range(HALF, NS):
        s_copy(s).start()
    for t in range(5, NT + 1):
        t_copy(t).start()

    def prepare_s(s):
        wide = blk[s, 0:32, :].astype(F32)
        turned = jnp.concatenate([wide[0:16] * (-2.0 * SCALE), wide[24:32] * SCALE, wide[16:24] * SCALE], axis=0)
        high, mid, low = pieces(turned)
        right[s, 0:32, :] = high.astype(BF16)
        right[s, 32:64, :] = mid.astype(BF16)
        right[s, 64:96, :] = low.astype(BF16)
        dir_s[s] = blk[s, 32:96, :]

    def prepare_t(slot):
        wide = blk[slot, 0:32, :].astype(F32)
        four = jnp.concatenate([wide, wide, wide, jnp.zeros_like(wide)], axis=0)
        left[...] = four.T.astype(BF16)

    def cross(x, s, half):
        for j in range(0, 512, WIDTH):
            x[j : j + WIDTH, :] = lax.dot_general(
                left[j : j + WIDTH, 0:96], right[s, :, half * WIDTH : (half + 1) * WIDTH],
                (((1,), (0,)), ((), ())), preferred_element_type=F32,
            )

    def fill(k, x):
        for j in range(0, 512, WIDTH):
            k[j : j + WIDTH, :] = entries(x[j : j + WIDTH, :])

    def add_s(k, s, half, slot):
        cols = slice(half * WIDTH, (half + 1) * WIDTH)
        acc_s[s, :, cols] += lax.dot_general(
            blk[slot, 32:96, :], k[...], (((1,), (0,)), ((), ())), preferred_element_type=F32
        )

    def add_t(k, s, half):
        cols = slice(half * WIDTH, (half + 1) * WIDTH)
        acc_t[...] += lax.dot_general(
            dir_s[s, :, cols], k[...], (((1,), (1,)), ((), ())), preferred_element_type=F32
        )

    acc_s[...] = jnp.zeros_like(acc_s)
    prepare_s(0)
    prepare_t(0)
    for half, (x, k) in enumerate(((x0, k0), (x1, k1))):
        cross(x, 0, half)
        fill(k, x)
        add_s(k, 0, half, 0)

    xs, ks = (x0, x1), (k0, k1)
    groups = HALF * 2

    def strip(h, t):
        slot = NS - 1 + t
        prepare_t(slot)
        acc_t[...] = jnp.zeros_like(acc_t)
        for g in range(groups + 2):
            if g < groups:
                cross(xs[g % 2], h * HALF + g // 2, g % 2)
            if g >= 2:
                add_s(ks[g % 2], h * HALF + (g - 2) // 2, g % 2, slot)
                add_t(ks[g % 2], h * HALF + (g - 2) // 2, g % 2)
            if 1 <= g <= groups:
                fill(ks[(g - 1) % 2], xs[(g - 1) % 2])

    def outer(h, carry):
        @pl.when(h == 0)
        def _():
            for s in range(1, HALF):
                s_copy(s).wait_recv()
                prepare_s(s)

        @pl.when(h == 1)
        def _():
            for s in range(1, HALF):
                out[s - 1] = acc_s[s].astype(BF16)
                out_copy(s - 1, s).start()
            for s in range(HALF, NS):
                s_copy(s).wait_recv()
                prepare_s(s)

        def inner(t, carry):
            @pl.when(h == 0)
            def _():
                t_copy(t).wait_recv()

                @pl.when(t == NT)
                def _():
                    dir_s[0] = jnp.zeros_like(dir_s[0])

            strip(h, t)

            @pl.when(h == 0)
            def _():
                part[t - 1] = acc_t[...]

            @pl.when(h == 1)
            def _():
                out[NS - 2 + t] = (acc_t[...] + part[t - 1]).astype(BF16)
                out_copy(NS - 2 + t, 8 * t).start()

            return carry

        return lax.fori_loop(1, NT + 1, inner, carry)

    lax.fori_loop(0, 2, outer, 0)
    for s in range(HALF, NS):
        out[s - 1] = acc_s[s].astype(BF16)
        out_copy(s - 1, s).start()

    res, dirn = residual[...], direction[...]
    total = acc_s[0]
    for slot in (0, 1, 2, 7, 8, 9, 10, 11, 12, 13, 3, 4, 5, 6, 14):
        out_copy(slot, 0).wait_recv()
        total = total + got[slot].astype(F32)
    image = total * FACTOR + dirn
    new_residual[...] = image

    def lanes(value):
        return jnp.sum(value, axis=1, keepdims=True)

    lane = lax.broadcasted_iota(jnp.int32, (64, 128), 1)
    table = jnp.where(lane == 0, lanes(res * res), 0.0)
    table = jnp.where(lane == 1, lanes(dirn * image), table)
    table = jnp.where(lane == 2, lanes(res * image), table)
    table = jnp.where(lane == 3, lanes(image * image), table)
    mine[...] = jnp.concatenate([table, jnp.zeros_like(table)], axis=0).T[0:8, :]

    def one_copy(s):
        return pltpu.make_async_remote_copy(
            src_ref=mine, dst_ref=one.at[s], send_sem=one_send.at[s], recv_sem=one_recv.at[s],
            device_id=device(-s), device_id_type=MESH,
        )

    def two_copy(t):
        return pltpu.make_async_remote_copy(
            src_ref=two.at[0], dst_ref=two.at[t], send_sem=two_send.at[t], recv_sem=two_recv.at[t],
            device_id=device(-8 * t), device_id_type=MESH,
        )

    for s in range(1, NS):
        one_copy(s).start()
    value = mine[...]
    for s in range(1, NS):
        one_copy(s).wait_recv()
        value = value + one[s]
    two[0] = value
    for t in range(1, 16):
        two_copy(t).start()
    for t in range(1, 16):
        two_copy(t).wait_recv()
        value = value + two[t]

    square = jnp.concatenate([value, jnp.zeros((120, 128), F32)], axis=0).T
    norm_old, curv = square[0:64, 0:1], square[0:64, 1:2]
    mixed, norm_image = square[0:64, 2:3], square[0:64, 3:4]
    alpha = norm_old / curv
    fresh = jnp.maximum(norm_old - alpha * (2.0 * mixed - alpha * norm_image), 0.0)
    beta = fresh / norm_old
    new_solution[...] = solution[...] + alpha * dirn
    updated = res - alpha * new_residual[...]
    new_residual[...] = updated
    new_direction[...] = updated + beta * dirn

    for s in range(1, NS):
        s_copy(s).wait_send()
        one_copy(s).wait_send()
    for t in range(1, NT + 1):
        t_copy(t).wait_send()
    for slot in range(15):
        out_copy(slot, 0).wait_send()
    for t in range(1, 16):
        two_copy(t).wait_send()


def local(coords, lengthscale, solution, residual, direction):
    probes, points = direction.shape
    big = jax.ShapeDtypeStruct((probes, points), F32)
    dma = pltpu.SemaphoreType.DMA
    return pl.pallas_call(
        kernel,
        out_shape=(big, big, big),
        in_specs=[pl.BlockSpec(memory_space=pltpu.VMEM)] * 5,
        out_specs=[pl.BlockSpec(memory_space=pltpu.VMEM)] * 3,
        scratch_shapes=[
            pltpu.VMEM((16, 96, 512), BF16),
            pltpu.VMEM((512, 128), BF16),
            pltpu.VMEM((NS, 96, 512), BF16),
            pltpu.VMEM((NS, 64, 512), BF16),
            pltpu.VMEM((NS, 64, 512), F32),
            pltpu.VMEM((64, 512), F32),
            pltpu.VMEM((15, 64, 512), BF16),
            pltpu.VMEM((15, 64, 512), BF16),
            pltpu.VMEM((512, WIDTH), F32),
            pltpu.VMEM((512, WIDTH), F32),
            pltpu.VMEM((512, WIDTH), BF16),
            pltpu.VMEM((512, WIDTH), BF16),
            pltpu.VMEM((8, 128), F32),
            pltpu.VMEM((NT, 64, 512), F32),
            pltpu.VMEM((NS, 8, 128), F32),
            pltpu.VMEM((16, 8, 128), F32),
            dma((16,)), dma((16,)), dma((15,)), dma((15,)), dma((8,)), dma((8,)), dma((16,)), dma((16,)),
        ],
        compiler_params=pltpu.CompilerParams(
            collective_id=0, has_side_effects=True, vmem_limit_bytes=48 * 2**20
        ),
    )(coords, lengthscale[:, None], solution, residual, direction)


def solution(mesh):
    spec = P(None, ("row", "col"))
    return jax.shard_map(
        local, mesh=mesh, in_specs=(spec, P(), spec, spec, spec), out_specs=(spec, spec, spec), check_vma=False
    )
```

```python
import math

import jax
import jax.numpy as jnp
from jax import lax
from jax.experimental import pallas as pl
from jax.experimental.pallas import tpu as pltpu
from jax.sharding import PartitionSpec as P

MESH = pl.DeviceIdType.MESH
F32 = jnp.float32
BF16 = jnp.bfloat16

NS = 8
NT = 8
NG = 16
HALF = 4
LN2 = math.log(2.0)
SCALE = 5.0 / LN2**2
SHIFT = 1.5 / LN2
CONST = 0.75 / LN2**2
FACTOR = LN2**2 / 3.0 * 2.0**SHIFT
WIDTH = 256


def entries(x, factor=None):
    t = jnp.maximum(x, 1e-12)
    w = -SHIFT - t * lax.rsqrt(t)
    value = (w * w + CONST) * jnp.exp2(w)
    return (value if factor is None else value * factor).astype(BF16)


def pieces(value):
    high = value.astype(BF16).astype(F32)
    mid = (value - high).astype(BF16).astype(F32)
    low = (value - high - mid).astype(BF16).astype(F32)
    return high, mid, low


def kernel(
    coords_hbm, scale_hbm, residual_hbm, direction_hbm, image_ref, coef_ref,
    coords, scale, residual, direction,
    blk, left, right, dir_s, acc_s, acc_t, out, got, x0, x1, k0, k1, mine, part, one, two,
    load, blk_send, blk_recv, out_send, out_recv, one_send, one_recv, two_send, two_recv,
):
    row, col = lax.axis_index("row"), lax.axis_index("col")
    core, y = row % 2, (row // 2) % 4
    z = (col // 4) * 2 + row // 8
    group = ((z + 2 * y) % 4) * 4 + y
    member = (col % 4) * 2 + core

    def device(dg, dm):
        g, m = (group + dg + NG) % NG, (member + dm + NS) % NS
        y = g % 4
        z = (2 * y + g // 4) % 4
        return ((z % 2) * 8 + y * 2 + m % 2, (z // 2) * 4 + m // 2)

    loads = [
        pltpu.make_async_copy(src, dst, load.at[i])
        for i, (src, dst) in enumerate(
            ((coords_hbm, coords), (scale_hbm, scale), (direction_hbm, direction), (residual_hbm, residual))
        )
    ]
    for copy in loads:
        copy.start()

    barrier = pltpu.get_barrier_semaphore()
    for s in range(1, NS):
        pl.semaphore_signal(barrier, inc=1, device_id=device(0, s), device_id_type=MESH)
    for t in range(1, NG):
        pl.semaphore_signal(barrier, inc=1, device_id=device(t, 0), device_id_type=MESH)

    def remote(src, dst, send, recv, dg, dm):
        return pltpu.make_async_remote_copy(
            src_ref=src, dst_ref=dst, send_sem=send, recv_sem=recv, device_id=device(dg, dm), device_id_type=MESH
        )

    def s_copy(s):
        return remote(blk.at[0], blk.at[s], blk_send.at[s], blk_recv.at[s], 0, s)

    def t_copy(t):
        slot = NS - 1 + t
        return remote(blk.at[0], blk.at[slot], blk_send.at[slot], blk_recv.at[slot], -t, 0)

    def out_copy(slot, dg, dm):
        return remote(out.at[slot], got.at[slot], out_send.at[slot], out_recv.at[slot], dg, dm)

    for copy in loads[0:3]:
        copy.wait()
    eye = lax.broadcasted_iota(jnp.int32, (16, 16), 0) == lax.broadcasted_iota(jnp.int32, (16, 16), 1)
    column = jnp.sum(jnp.where(eye, jnp.broadcast_to(scale[...], (16, 16)), 0.0), axis=1, keepdims=True)
    blk[0, 0:16, :] = (coords[...] / column).astype(BF16)
    blk[0, 16:80, :] = direction[...].astype(BF16)

    pl.semaphore_wait(barrier, NS - 1 + NG - 1)
    for s in range(1, HALF):
        s_copy(s).start()
    for t in (4, 5, 6):
        t_copy(t).start()
    for s in range(HALF, NS):
        s_copy(s).start()
    for t in (7, 1, 2, 3, 8):
        t_copy(t).start()

    def features(slot):
        wide = blk[slot, 0:16, :].astype(F32)
        high, mid, low = pieces(jnp.sum(wide * wide, axis=0, keepdims=True))
        rows = lax.broadcasted_iota(jnp.int32, (8, 512), 0)
        norm = jnp.where(rows == 0, high, jnp.where(rows == 1, mid, jnp.where(rows == 2, low, 0.0)))
        return wide, norm, jnp.where(rows < 3, 1.0, 0.0)

    def prepare_s(s):
        wide, norm, ones = features(s)
        turned = jnp.concatenate([wide * (-2.0 * SCALE), ones * SCALE, norm * SCALE], axis=0)
        high, mid, low = pieces(turned)
        right[s, 0:32, :] = high.astype(BF16)
        right[s, 32:64, :] = mid.astype(BF16)
        right[s, 64:96, :] = low.astype(BF16)
        dir_s[s] = blk[s, 16:80, :]

    def prepare_t(slot):
        wide, norm, ones = features(slot)
        one_set = jnp.concatenate([wide, norm, ones], axis=0)
        four = jnp.concatenate([one_set, one_set, one_set, jnp.zeros_like(one_set)], axis=0)
        left[...] = four.T.astype(BF16)

    def cross(x, s, half):
        for j in range(0, 512, WIDTH):
            x[j : j + WIDTH, :] = lax.dot_general(
                left[j : j + WIDTH, 0:96], right[s, :, half * WIDTH : (half + 1) * WIDTH],
                (((1,), (0,)), ((), ())), preferred_element_type=F32,
            )

    def fill(k, x, factor=None):
        for j in range(0, 512, WIDTH):
            k[j : j + WIDTH, :] = entries(x[j : j + WIDTH, :], factor)

    def add_s(k, s, half, slot):
        cols = slice(half * WIDTH, (half + 1) * WIDTH)
        acc_s[s, :, cols] += lax.dot_general(
            blk[slot, 16:80, :], k[...], (((1,), (0,)), ((), ())), preferred_element_type=F32
        )

    def add_t(k, s, half):
        cols = slice(half * WIDTH, (half + 1) * WIDTH)
        acc_t[...] += lax.dot_general(
            dir_s[s, :, cols], k[...], (((1,), (1,)), ((), ())), preferred_element_type=F32
        )

    xs, ks = (x0, x1), (k0, k1)

    def strip(base, sides, slot):
        prepare_t(slot)
        acc_t[...] = jnp.zeros_like(acc_t)
        groups = 2 * len(sides)
        for g in range(groups + 2):
            if g < groups:
                cross(xs[g % 2], base + g // 2, g % 2)
            if g >= 2:
                add_s(ks[g % 2], base + (g - 2) // 2, g % 2, slot)
                if sides[(g - 2) // 2]:
                    add_t(ks[g % 2], base + (g - 2) // 2, g % 2)
            if 1 <= g <= groups:
                fill(ks[(g - 1) % 2], xs[(g - 1) % 2])

    acc_s[...] = jnp.zeros_like(acc_s)
    prepare_s(0)
    prepare_t(0)
    for half in range(2):
        cross(xs[half], 0, half)
        fill(ks[half], xs[half], FACTOR)
        add_s(ks[half], 0, half, 0)
    acc_s[0] = acc_s[0] * (1.0 / FACTOR)

    def first(i, carry):
        t = (i + 3) % 7 + 1
        t_copy(t).wait_recv()
        strip(0, (True,) * HALF, NS - 1 + t)
        part[t - 1] = acc_t[...]
        return carry

    def middle(u, carry):
        strip(1, (True, True, True, False), u * 15)

        @pl.when(u == 0)
        def _():
            acc_s[0] += acc_t[...]

        return carry

    def second(i, carry):
        t = (i + 4) % 7 + 1
        strip(HALF, (True,) * HALF, NS - 1 + t)
        out[NS - 2 + t] = (acc_t[...] + part[t - 1]).astype(BF16)
        out_copy(NS - 2 + t, t, 0).start()
        return carry

    def send_s(s):
        out[s - 1] = acc_s[s].astype(BF16)
        out_copy(s - 1, 0, -s).start()

    for s in range(1, HALF):
        s_copy(s).wait_recv()
        prepare_s(s)
    lax.fori_loop(0, 7, first, 0)
    for s in range(HALF, NS):
        s_copy(s).wait_recv()
        prepare_s(s)
    t_copy(8).wait_recv()
    lax.fori_loop(0, 2, middle, 0)
    out[14] = acc_t[...].astype(BF16)
    out_copy(14, 8, 0).start()
    for s in range(1, HALF):
        send_s(s)
    lax.fori_loop(0, 7, second, 0)
    for s in range(HALF, NS):
        send_s(s)
    prepare_t(15)
    for half in range(2):
        cross(xs[half], 0, half)
        fill(ks[half], xs[half])
        add_s(ks[half], 0, half, 15)

    loads[3].wait()
    res, dirn = residual[...], direction[...]
    total = acc_s[0]
    for slot in (0, 1, 2, 14, 11, 12, 13, 7, 8, 9, 10, 3, 4, 5, 6):
        out_copy(slot, 0, 0).wait_recv()
        total = total + got[slot].astype(F32)
    image = total * FACTOR + dirn
    image_ref[...] = image

    def lanes(value):
        return jnp.sum(value, axis=1, keepdims=True)

    lane = lax.broadcasted_iota(jnp.int32, (64, 128), 1)
    table = jnp.where(lane == 0, lanes(res * res), 0.0)
    table = jnp.where(lane == 1, lanes(dirn * image), table)
    table = jnp.where(lane == 2, lanes(res * image), table)
    table = jnp.where(lane == 3, lanes(image * image), table)
    mine[...] = jnp.concatenate([table, jnp.zeros_like(table)], axis=0).T[0:8, :]

    def one_copy(s):
        return remote(mine, one.at[s], one_send.at[s], one_recv.at[s], 0, s)

    def two_copy(t):
        return remote(two.at[0], two.at[t], two_send.at[t], two_recv.at[t], t, 0)

    for s in range(1, NS):
        one_copy(s).start()
    value = mine[...]
    for s in range(1, NS):
        one_copy(s).wait_recv()
        value = value + one[s]
    two[0] = value
    for t in range(1, NG):
        two_copy(t).start()
    for t in range(1, NG):
        two_copy(t).wait_recv()
        value = value + two[t]

    square = jnp.concatenate([value, jnp.zeros((120, 128), F32)], axis=0).T
    norm_old, curv = square[0:64, 0:1], square[0:64, 1:2]
    mixed, norm_image = square[0:64, 2:3], square[0:64, 3:4]
    alpha = norm_old / curv
    fresh = jnp.maximum(norm_old - alpha * (2.0 * mixed - alpha * norm_image), 0.0)
    beta = fresh / norm_old
    coef_ref[...] = jnp.where(lane == 0, alpha, jnp.where(lane == 1, beta, 0.0))

    for s in range(1, NS):
        s_copy(s).wait_send()
        one_copy(s).wait_send()
    for t in range(1, NT + 1):
        t_copy(t).wait_send()
    for slot in range(15):
        out_copy(slot, 0, 0).wait_send()
    for t in range(1, NG):
        two_copy(t).wait_send()


def local(coords, lengthscale, solution, residual, direction):
    probes, points = direction.shape
    feats = coords.shape[0]
    dma = pltpu.SemaphoreType.DMA
    image, coef = pl.pallas_call(
        kernel,
        out_shape=(jax.ShapeDtypeStruct((probes, points), F32), jax.ShapeDtypeStruct((probes, 128), F32)),
        in_specs=[pl.BlockSpec(memory_space=pl.ANY)] * 4,
        out_specs=[pl.BlockSpec(memory_space=pltpu.VMEM)] * 2,
        scratch_shapes=[
            pltpu.VMEM((feats, points), F32),
            pltpu.VMEM((1, feats), F32),
            pltpu.VMEM((probes, points), F32),
            pltpu.VMEM((probes, points), F32),
            pltpu.VMEM((16, 80, 512), BF16),
            pltpu.VMEM((512, 128), BF16),
            pltpu.VMEM((NS, 96, 512), BF16),
            pltpu.VMEM((NS, 64, 512), BF16),
            pltpu.VMEM((NS, 64, 512), F32),
            pltpu.VMEM((64, 512), F32),
            pltpu.VMEM((15, 64, 512), BF16),
            pltpu.VMEM((15, 64, 512), BF16),
            pltpu.VMEM((512, WIDTH), F32),
            pltpu.VMEM((512, WIDTH), F32),
            pltpu.VMEM((512, WIDTH), BF16),
            pltpu.VMEM((512, WIDTH), BF16),
            pltpu.VMEM((8, 128), F32),
            pltpu.VMEM((NT, 64, 512), F32),
            pltpu.VMEM((NS, 8, 128), F32),
            pltpu.VMEM((NG, 8, 128), F32),
            dma((4,)), dma((16,)), dma((16,)), dma((15,)), dma((15,)), dma((8,)), dma((8,)), dma((16,)), dma((16,)),
        ],
        compiler_params=pltpu.CompilerParams(
            collective_id=0, has_side_effects=True, vmem_limit_bytes=48 * 2**20
        ),
    )(coords, lengthscale[None, :], residual, direction)
    alpha, beta = coef[:, 0:1], coef[:, 1:2]
    new_residual = residual - alpha * image
    return solution + alpha * direction, new_residual, new_residual + beta * direction


def solution(mesh):
    spec = P(None, ("row", "col"))
    return jax.shard_map(
        local, mesh=mesh, in_specs=(spec, P(), spec, spec, spec), out_specs=(spec, spec, spec), check_vma=False
    )
```

```python
import math

import jax
import jax.numpy as jnp
from jax import lax
from jax.experimental import pallas as pl
from jax.experimental.pallas import tpu as pltpu
from jax.sharding import PartitionSpec as P

MESH = pl.DeviceIdType.MESH
F32 = jnp.float32
BF16 = jnp.bfloat16

NS = 8
NT = 8
NG = 16
HALF = 4
LN2 = math.log(2.0)
SCALE = 5.0 / LN2**2
SHIFT = 1.5 / LN2
CONST = 0.75 / LN2**2
FACTOR = LN2**2 / 3.0 * 2.0**SHIFT
WIDTH = 256
VMEM = 60 * 2**20


def entries(x, factor=None):
    t = jnp.maximum(x, 1e-12)
    w = -SHIFT - t * lax.rsqrt(t)
    value = (w * w + CONST) * jnp.exp2(w)
    return (value if factor is None else value * factor).astype(BF16)


def pieces(value):
    high = value.astype(BF16).astype(F32)
    mid = (value - high).astype(BF16).astype(F32)
    low = (value - high - mid).astype(BF16).astype(F32)
    return high, mid, low


def kernel(
    coords_hbm, scale_hbm, residual_hbm, direction_hbm, image_ref, coef_ref,
    coords, scale, residual, direction,
    blk, left, right, dir_s, acc, out, got, x0, x1, k0, k1, mine, one, two,
    load, blk_send, blk_recv, out_send, out_recv, one_send, one_recv, two_send, two_recv,
):
    row, col = lax.axis_index("row"), lax.axis_index("col")
    core, y, z_lo = lax.rem(row, 2), lax.rem(lax.div(row, 2), 4), lax.div(row, 8)
    x, z_hi = lax.rem(col, 4), lax.div(col, 4)
    group = lax.rem(z_hi * 2 + z_lo + 2 * y, 4) * 4 + y
    member = core * 4 + x

    ring = {}
    for s in range(1, NS):
        m = lax.rem(member + s, NS)
        ring[s] = (row - core + lax.div(m, 4), z_hi * 4 + lax.rem(m, 4))

    def across(t):
        g = lax.rem(group + t, NG)
        to_y = lax.rem(g, 4)
        to_z = lax.rem(2 * to_y + lax.div(g, 4), 4)
        return (lax.rem(to_z, 2) * 8 + to_y * 2 + core, lax.div(to_z, 2) * 4 + x)

    plane = {t: across(t) for t in range(1, NG)}

    loads = [
        pltpu.make_async_copy(src, dst, load.at[i])
        for i, (src, dst) in enumerate(
            ((coords_hbm, coords), (scale_hbm, scale), (direction_hbm, direction), (residual_hbm, residual))
        )
    ]
    for copy in loads:
        copy.start()

    barrier = pltpu.get_barrier_semaphore()
    for s in range(1, NS):
        pl.semaphore_signal(barrier, inc=1, device_id=ring[s], device_id_type=MESH)
    for t in range(1, NG):
        pl.semaphore_signal(barrier, inc=1, device_id=plane[t], device_id_type=MESH)

    def remote(src, dst, send, recv, where):
        return pltpu.make_async_remote_copy(
            src_ref=src, dst_ref=dst, send_sem=send, recv_sem=recv, device_id=where, device_id_type=MESH
        )

    def s_copy(s):
        return remote(blk.at[0], blk.at[s], blk_send.at[s], blk_recv.at[s], ring[s])

    def t_copy(t, where=None):
        slot = NS + t
        return remote(blk.at[0], blk.at[slot], blk_send.at[slot], blk_recv.at[slot], where or ring[1])

    def out_copy(slot, where=None):
        return remote(out.at[slot], got.at[slot], out_send.at[slot], out_recv.at[slot], where or ring[1])

    for copy in loads[0:3]:
        copy.wait()
    eye = lax.broadcasted_iota(jnp.int32, (16, 16), 0) == lax.broadcasted_iota(jnp.int32, (16, 16), 1)
    column = jnp.sum(jnp.where(eye, jnp.broadcast_to(scale[...], (16, 16)), 0.0), axis=1, keepdims=True)
    blk[0, 0:16, :] = (coords[...] / column).astype(BF16)
    blk[0, 16:80, :] = direction[...].astype(BF16)
    blk[NS] = blk[0]

    def features(slot):
        wide = blk[slot, 0:16, :].astype(F32)
        high, mid, low = pieces(jnp.sum(wide * wide, axis=0, keepdims=True))
        rows = lax.broadcasted_iota(jnp.int32, (8, 512), 0)
        norm = jnp.where(rows == 0, high, jnp.where(rows == 1, mid, jnp.where(rows == 2, low, 0.0)))
        return wide, norm, jnp.where(rows < 3, 1.0, 0.0)

    def prepare_s(s):
        wide, norm, ones = features(s)
        one_set = jnp.concatenate([wide, norm, ones], axis=0)
        four = jnp.concatenate([one_set, one_set, one_set, jnp.zeros_like(one_set)], axis=0)
        left[s] = four.T.astype(BF16)
        dir_s[s] = blk[s, 16:80, :]

    def prepare_t(t):
        wide, norm, ones = features(NS + t)
        turned = jnp.concatenate([wide * (-2.0 * SCALE), ones * SCALE, norm * SCALE], axis=0)
        high, mid, low = pieces(turned)
        right[t, 0:32, :] = high.astype(BF16)
        right[t, 32:64, :] = mid.astype(BF16)
        right[t, 64:96, :] = low.astype(BF16)

    def cross(x, s, t, half):
        for j in range(0, 512, WIDTH):
            x[j : j + WIDTH, :] = lax.dot_general(
                left[s, j : j + WIDTH, 0:96], right[t, :, half * WIDTH : (half + 1) * WIDTH],
                (((1,), (0,)), ((), ())), preferred_element_type=F32,
            )

    def fill(k, x, half, factor=None):
        for j in range(0, 512, WIDTH):
            k[j : j + WIDTH, half * WIDTH : (half + 1) * WIDTH] = entries(x[j : j + WIDTH, :], factor)

    def to_t(k, s, t):
        acc[NS + t] += lax.dot_general(dir_s[s], k[...], (((1,), (0,)), ((), ())), preferred_element_type=F32)

    def to_s(k, s, t):
        acc[s] += lax.dot_general(
            blk[NS + t, 16:80, :], k[...], (((1,), (1,)), ((), ())), preferred_element_type=F32
        )

    acc[...] = jnp.zeros_like(acc)
    k1[...] = jnp.zeros_like(k1)
    dir_s[NS] = jnp.zeros_like(dir_s[NS])
    prepare_s(0)
    prepare_t(0)
    cross(x0, 0, 0, 0)
    cross(x1, 0, 0, 1)
    fill(k0, x0, 0, FACTOR)
    fill(k0, x1, 1, FACTOR)
    to_s(k0, 0, 0)
    acc[0] = acc[0] * (1.0 / FACTOR)

    pl.semaphore_wait(barrier, NS - 1 + NG - 1)
    for s in (4, 1, 3, 2):
        s_copy(s).start()
    for t in (4, 5, 6):
        t_copy(t, plane[NG - t]).start()


    def plan(q):
        late = q > 8
        t = jnp.where(late, lax.rem(lax.max(q - 9, 0) + 4, 7) + 1, lax.rem(q + 2, 7) + 1)
        t = jnp.where(q == 8, 8, t)
        base = jnp.where(q == 8, 1, jnp.where(late, HALF, 0))
        slots = [base, base + 1, base + 2, base + 3]
        return t, slots, slots[0:3] + [jnp.where(q == 8, NS, base + 3)]

    ks = (k0, k1)

    def slot_step(i, now, old, following):
        (s, t), (old_s, old_dir, old_t) = now, old
        cross(x1, s, t, 1)
        to_t(ks[1 - i % 2], old_dir, old_t)
        fill(ks[i % 2], x0, 0)
        if following is not None:
            cross(x0, following[0], following[1], 0)
        to_s(ks[1 - i % 2], old_s, old_t)
        fill(ks[i % 2], x1, 1)

    def strip(q, carry):
        t, slots, dirs = plan(q)
        before_t, before_slots, before_dirs = plan(q - 1)
        before_t = jnp.where(q == 1, 0, before_t)
        before_slots = before_slots[0:3] + [jnp.where(q == 1, 2, before_slots[3])]
        before_dirs = before_dirs[0:3] + [jnp.where(q == 1, 2, before_dirs[3])]
        after_t, after_slots, _ = plan(q + 1)
        after_slots = [jnp.where(q == 13, 5, after_slots[0])]

        @pl.when(q < 7)
        def _():
            t_copy(after_t).wait_recv()
            prepare_t(after_t)

        @pl.when(q < 4)
        def _():
            later = lax.rem(q + 6, 7) + 1
            t_copy(later, across(NG - later)).start()

        @pl.when(q == 1)
        def _():
            for s in (5, 7, 6):
                s_copy(s).start()

        @pl.when(q == 4)
        def _():
            t_copy(8, plane[8]).start()

        @pl.when(q == 7)
        def _():
            t_copy(8).wait_recv()
            prepare_t(8)
            for s in range(HALF + 1, NS):
                s_copy(s).wait_recv()
                prepare_s(s)

        old = (before_slots[3], before_dirs[3], before_t)
        for i in range(4):
            following = (after_slots[0], after_t) if i == 3 else (slots[i + 1], t)
            slot_step(i, (slots[i], t), old, following)
            old = (slots[i], dirs[i], t)

        @pl.when(q == 9)
        def _():
            send_t(8, plane[8])
            for s in range(1, HALF):
                send_s(s)

        @pl.when(q > 9)
        def _():
            send_t(before_t, across(before_t))

        return carry

    def send_t(t, where):
        out[NS - 2 + t] = acc[NS + t].astype(BF16)
        out_copy(NS - 2 + t, where).start()

    def send_s(s):
        out[s - 1] = acc[s].astype(BF16)
        out_copy(s - 1, ring[NS - s]).start()

    old = (1, NS, 0)
    order = (4, 1, 3, 2)
    for i, s in enumerate(order):
        if i == 0:
            s_copy(s).wait_recv()
            prepare_s(s)
            cross(x0, s, 0, 0)
        if i < 3:
            s_copy(order[i + 1]).wait_recv()
            prepare_s(order[i + 1])
            following = (order[i + 1], 0)
        else:
            t_copy(4).wait_recv()
            prepare_t(4)
            following = (0, 4)
        slot_step(i, (s, 0), old, following)
        old = (s, NS if s == HALF else s, 0)
    t_copy(7, plane[NG - 7]).start()
    lax.fori_loop(1, 14, strip, 0)
    order = [(s, t) for s in (5, 6, 7, 4) for t in (3, 4)]
    old = (7, 7, 2)
    for i, (s, t) in enumerate(order):
        slot_step(i, (s, t), old, order[i + 1] if i < 7 else None)
        if i == 0:
            send_t(2, plane[2])
        elif i % 2 == 0:
            send_s(order[i - 1][0])
        old = (s, s, t)
    send_t(3, plane[3])
    to_t(k1, 4, 4)
    send_t(4, plane[4])
    to_s(k1, 4, 4)
    send_s(4)
    cross(x0, 0, 8, 0)
    cross(x1, 0, 8, 1)
    fill(k0, x0, 0)
    fill(k0, x1, 1)
    to_s(k0, 0, 8)

    loads[3].wait()
    res, dirn = residual[...], direction[...]
    total = acc[0] + acc[NS]
    for slot in (0, 1, 2, 14, 11, 12, 13, 7, 8, 4, 5, 6, 9, 3, 10):
        out_copy(slot).wait_recv()
        total = total + got[slot].astype(F32)
    image = total * FACTOR + dirn
    image_ref[...] = image

    def lanes(value):
        return jnp.sum(value, axis=1, keepdims=True)

    lane = lax.broadcasted_iota(jnp.int32, (64, 128), 1)
    table = jnp.where(lane == 0, lanes(res * res), 0.0)
    table = jnp.where(lane == 1, lanes(dirn * image), table)
    table = jnp.where(lane == 2, lanes(res * image), table)
    table = jnp.where(lane == 3, lanes(image * image), table)
    mine[...] = jnp.concatenate([table, jnp.zeros_like(table)], axis=0).T[0:8, :]

    def one_copy(s):
        return remote(mine, one.at[s], one_send.at[s], one_recv.at[s], ring[s])

    def two_copy(t):
        return remote(two.at[0], two.at[t], two_send.at[t], two_recv.at[t], plane[t])

    for s in range(1, NS):
        one_copy(s).start()
    value = mine[...]
    for s in range(1, NS):
        one_copy(s).wait_recv()
        value = value + one[s]
    two[0] = value
    for t in range(1, NG):
        two_copy(t).start()
    for t in range(1, NG):
        two_copy(t).wait_recv()
        value = value + two[t]

    square = jnp.concatenate([value, jnp.zeros((120, 128), F32)], axis=0).T
    norm_old, curv = square[0:64, 0:1], square[0:64, 1:2]
    mixed, norm_image = square[0:64, 2:3], square[0:64, 3:4]
    alpha = norm_old / curv
    fresh = jnp.maximum(norm_old - alpha * (2.0 * mixed - alpha * norm_image), 0.0)
    beta = fresh / norm_old
    coef_ref[...] = jnp.where(lane == 0, alpha, jnp.where(lane == 1, beta, 0.0))

    for s in range(1, NS):
        s_copy(s).wait_send()
        one_copy(s).wait_send()
    for t in range(1, NT + 1):
        t_copy(t).wait_send()
    for slot in range(15):
        out_copy(slot).wait_send()
    for t in range(1, NG):
        two_copy(t).wait_send()


def local(coords, lengthscale, solution, residual, direction):
    probes, points = direction.shape
    feats = coords.shape[0]
    dma = pltpu.SemaphoreType.DMA
    image, coef = pl.pallas_call(
        kernel,
        out_shape=(jax.ShapeDtypeStruct((probes, points), F32), jax.ShapeDtypeStruct((probes, 128), F32)),
        in_specs=[pl.BlockSpec(memory_space=pl.ANY)] * 4,
        out_specs=[pl.BlockSpec(memory_space=pltpu.VMEM)] * 2,
        scratch_shapes=[
            pltpu.VMEM((feats, points), F32),
            pltpu.VMEM((1, feats), F32),
            pltpu.VMEM((probes, points), F32),
            pltpu.VMEM((probes, points), F32),
            pltpu.VMEM((17, 80, 512), BF16),
            pltpu.VMEM((NS, 512, 128), BF16),
            pltpu.VMEM((NT + 1, 96, 512), BF16),
            pltpu.VMEM((NS + 1, 64, 512), BF16),
            pltpu.VMEM((17, 64, 512), F32),
            pltpu.VMEM((15, 64, 512), BF16),
            pltpu.VMEM((15, 64, 512), BF16),
            pltpu.VMEM((512, WIDTH), F32),
            pltpu.VMEM((512, WIDTH), F32),
            pltpu.VMEM((512, 512), BF16),
            pltpu.VMEM((512, 512), BF16),
            pltpu.VMEM((8, 128), F32),
            pltpu.VMEM((NS, 8, 128), F32),
            pltpu.VMEM((NG, 8, 128), F32),
            dma((4,)), dma((17,)), dma((17,)), dma((15,)), dma((15,)), dma((8,)), dma((8,)), dma((16,)), dma((16,)),
        ],
        compiler_params=pltpu.CompilerParams(
            collective_id=0, has_side_effects=True, vmem_limit_bytes=VMEM
        ),
    )(coords, lengthscale[None, :], residual, direction)
    alpha, beta = coef[:, 0:1], coef[:, 1:2]
    new_residual = residual - alpha * image
    return solution + alpha * direction, new_residual, new_residual + beta * direction


def solution(mesh):
    spec = P(None, ("row", "col"))
    return jax.shard_map(
        local, mesh=mesh, in_specs=(spec, P(), spec, spec, spec), out_specs=(spec, spec, spec), check_vma=False
    )
```

```python
import math

import jax
import jax.numpy as jnp
from jax import lax
from jax.experimental import pallas as pl
from jax.experimental.pallas import tpu as pltpu
from jax.sharding import PartitionSpec as P

MESH = pl.DeviceIdType.MESH
F32 = jnp.float32
BF16 = jnp.bfloat16

NS = 8
NT = 8
NG = 16
HALF = 4
LN2 = math.log(2.0)
SCALE = 5.0 / LN2**2
SHIFT = 1.5 / LN2
CONST = 0.75 / LN2**2
FACTOR = LN2**2 / 3.0 * 2.0**SHIFT
WIDTH = 256
VMEM = 60 * 2**20


def entries(x, factor=None):
    w = -SHIFT - x * lax.rsqrt(x)
    value = (w * w + CONST) * jnp.exp2(w)
    return (value if factor is None else value * factor).astype(BF16)


def pieces(value):
    high = value.astype(BF16).astype(F32)
    mid = (value - high).astype(BF16).astype(F32)
    low = (value - high - mid).astype(BF16).astype(F32)
    return high, mid, low


def kernel(
    coords_hbm, scale_hbm, residual_hbm, direction_hbm, image_ref, alpha_ref, beta_ref,
    coords, scale, residual, direction,
    blk, left, right, dir_s, acc, out, got, x0, x1, k0, k1, mine, one, two,
    load, blk_send, blk_recv, out_send, out_recv, one_send, one_recv, two_send, two_recv,
):
    row, col = lax.axis_index("row"), lax.axis_index("col")
    core, y, z_lo = lax.rem(row, 2), lax.rem(lax.div(row, 2), 4), lax.div(row, 8)
    x, z_hi = lax.rem(col, 4), lax.div(col, 4)
    group = lax.rem(z_hi * 2 + z_lo + 2 * y, 4) * 4 + y
    member = core * 4 + x

    ring = {}
    for s in range(1, NS):
        m = lax.rem(member + s, NS)
        ring[s] = (row - core + lax.div(m, 4), z_hi * 4 + lax.rem(m, 4))

    def across(t):
        g = lax.rem(group + t, NG)
        to_y = lax.rem(g, 4)
        to_z = lax.rem(2 * to_y + lax.div(g, 4), 4)
        return (lax.rem(to_z, 2) * 8 + to_y * 2 + core, lax.div(to_z, 2) * 4 + x)

    plane = {t: across(t) for t in range(1, NG)}

    loads = [
        pltpu.make_async_copy(src, dst, load.at[i])
        for i, (src, dst) in enumerate(
            ((coords_hbm, coords), (scale_hbm, scale), (direction_hbm, direction), (residual_hbm, residual))
        )
    ]
    for copy in loads:
        copy.start()

    barrier = pltpu.get_barrier_semaphore()
    for s in range(1, NS):
        pl.semaphore_signal(barrier, inc=1, device_id=ring[s], device_id_type=MESH)
    for t in range(1, NG):
        pl.semaphore_signal(barrier, inc=1, device_id=plane[t], device_id_type=MESH)

    def remote(src, dst, send, recv, where):
        return pltpu.make_async_remote_copy(
            src_ref=src, dst_ref=dst, send_sem=send, recv_sem=recv, device_id=where, device_id_type=MESH
        )

    def s_copy(s):
        return remote(blk.at[0], blk.at[s], blk_send.at[s], blk_recv.at[s], ring[s])

    def t_copy(t, where=None):
        slot = NS + t
        return remote(blk.at[0], blk.at[slot], blk_send.at[slot], blk_recv.at[slot], where or ring[1])

    def out_copy(slot, where=None):
        return remote(out.at[slot], got.at[slot], out_send.at[slot], out_recv.at[slot], where or ring[1])

    for copy in loads[0:3]:
        copy.wait()
    eye = lax.broadcasted_iota(jnp.int32, (16, 16), 0) == lax.broadcasted_iota(jnp.int32, (16, 16), 1)
    column = jnp.sum(jnp.where(eye, jnp.broadcast_to(scale[...], (16, 16)), 0.0), axis=1, keepdims=True)
    blk[0, 0:16, :] = (coords[...] / column).astype(BF16)
    blk[0, 16:80, :] = direction[...].astype(BF16)
    blk[NS] = blk[0]

    def features(slot):
        wide = blk[slot, 0:16, :].astype(F32)
        high, mid, low = pieces(jnp.sum(wide * wide, axis=0, keepdims=True))
        rows = lax.broadcasted_iota(jnp.int32, (8, 512), 0)
        norm = jnp.where(rows == 0, high, jnp.where(rows == 1, mid, jnp.where(rows == 2, low, 0.0)))
        return wide, norm, jnp.where(rows < 3, 1.0, 0.0)

    def prepare_s(s):
        wide, norm, ones = features(s)
        one_set = jnp.concatenate([wide, norm, ones], axis=0)
        four = jnp.concatenate([one_set, one_set, one_set, jnp.zeros_like(one_set)], axis=0)
        left[s] = four.T.astype(BF16)
        dir_s[s] = blk[s, 16:80, :]

    def prepare_t(t):
        wide, norm, ones = features(NS + t)
        turned = jnp.concatenate([wide * (-2.0 * SCALE), ones * SCALE, norm * SCALE], axis=0)
        high, mid, low = pieces(turned)
        right[t, 0:32, :] = high.astype(BF16)
        right[t, 32:64, :] = mid.astype(BF16)
        right[t, 64:96, :] = low.astype(BF16)

    def cross(x, s, t, half):
        for j in range(0, 512, WIDTH):
            dist = lax.dot_general(
                left[s, j : j + WIDTH, 0:96], right[t, :, half * WIDTH : (half + 1) * WIDTH],
                (((1,), (0,)), ((), ())), preferred_element_type=F32,
            )
            x[j : j + WIDTH, :] = jnp.maximum(dist, 1e-12)

    def fill(k, x, factor=None):
        for j in range(0, 512, WIDTH):
            k[j : j + WIDTH, :] = entries(x[j : j + WIDTH, :], factor)

    def to_t(half, s, t):
        acc[NS + t, :, half * WIDTH : (half + 1) * WIDTH] += lax.dot_general(
            dir_s[s], (k0, k1)[half][...], (((1,), (0,)), ((), ())), preferred_element_type=F32
        )

    def to_s(half, s, t):
        acc[s] += lax.dot_general(
            blk[NS + t, 16:80, half * WIDTH : (half + 1) * WIDTH], (k0, k1)[half][...],
            (((1,), (1,)), ((), ())), preferred_element_type=F32,
        )

    acc[...] = jnp.zeros_like(acc)
    dir_s[NS] = jnp.zeros_like(dir_s[NS])
    prepare_s(0)
    prepare_t(0)
    cross(x0, 0, 0, 0)
    cross(x1, 0, 0, 1)
    fill(k0, x0, FACTOR)
    fill(k1, x1, FACTOR)
    to_s(0, 0, 0)
    to_s(1, 0, 0)
    acc[0] = acc[0] * (1.0 / FACTOR)
    k1[...] = jnp.zeros_like(k1)

    pl.semaphore_wait(barrier, NS - 1 + NG - 1)
    for s in (4, 1, 3):
        s_copy(s).start()
    t_copy(4, plane[NG - 4]).start()


    def plan(q):
        late = q > 8
        t = lax.rem(jnp.where(late, 2 * q + 1, 5 * q + 5), 7) + 1
        t = jnp.where(q == 8, 8, t)
        base = jnp.where(q == 8, 1, jnp.where(late, HALF, 0))
        slots = [base, base + 1, base + 2, base + 3]
        return t, slots, slots[0:3] + [jnp.where(q == 8, NS, base + 3)]

    def block(now, old, following):
        (s, dir_of, t), (old_s, old_dir, old_t) = now, old
        to_t(1, old_dir, old_t)
        cross(x1, s, t, 1)
        to_s(1, old_s, old_t)
        fill(k0, x0)
        to_t(0, dir_of, t)
        if following is not None:
            cross(x0, following[0], following[1], 0)
        to_s(0, s, t)
        fill(k1, x1)

    def strip(q, carry):
        t, slots, dirs = plan(q)
        before_t, before_slots, before_dirs = plan(q - 1)
        before_t = jnp.where(q == 1, 0, before_t)
        before_slots = before_slots[0:3] + [jnp.where(q == 1, 2, before_slots[3])]
        before_dirs = before_dirs[0:3] + [jnp.where(q == 1, 2, before_dirs[3])]
        after_t, after_slots, _ = plan(q + 1)
        after_slots = [jnp.where(q == 13, 5, after_slots[0])]

        @pl.when(q < 7)
        def _():
            t_copy(after_t).wait_recv()
            prepare_t(after_t)

        @pl.when(q < 4)
        def _():
            later = lax.rem(5 * q + 4, 7) + 1
            t_copy(later, across(NG - later)).start()

        @pl.when(q == 1)
        def _():
            for s in (5, 7, 6):
                s_copy(s).start()

        @pl.when(q == 4)
        def _():
            t_copy(8, plane[8]).start()

        @pl.when(q == 7)
        def _():
            t_copy(8).wait_recv()
            prepare_t(8)
            for s in range(HALF + 1, NS):
                s_copy(s).wait_recv()
                prepare_s(s)

        old = (before_slots[3], before_dirs[3], before_t)
        for i in range(4):
            following = (after_slots[0], after_t) if i == 3 else (slots[i + 1], t)
            block((slots[i], dirs[i], t), old, following)
            old = (slots[i], dirs[i], t)

        @pl.when(q == 9)
        def _():
            send_t(8, plane[8])
            for s in range(1, HALF):
                send_s(s)

        @pl.when(q > 9)
        def _():
            send_t(before_t, across(before_t))

        return carry

    def send_t(t, where):
        out[NS - 2 + t] = acc[NS + t].astype(BF16)
        out_copy(NS - 2 + t, where).start()

    def send_s(s):
        out[s - 1] = acc[s].astype(BF16)
        out_copy(s - 1, ring[NS - s]).start()

    old = (1, NS, 0)
    order = (4, 1, 3, 2)
    for i, s in enumerate(order):
        if i == 0:
            s_copy(s).wait_recv()
            s_copy(2).start()
            t_copy(2, plane[NG - 2]).start()
            prepare_s(s)
            cross(x0, s, 0, 0)
        if i < 3:
            s_copy(order[i + 1]).wait_recv()
            prepare_s(order[i + 1])
            following = (order[i + 1], 0)
        else:
            t_copy(4).wait_recv()
            prepare_t(4)
            following = (0, 4)
        if i == 1:
            t_copy(7, plane[NG - 7]).start()
        now = (s, NS if s == HALF else s, 0)
        block(now, old, following)
        old = now
    t_copy(5, plane[NG - 5]).start()
    lax.fori_loop(1, 14, strip, 0)
    order = [(s, t) for s in (5, 6, 7, 4) for t in (2, 4)]
    old = (7, 7, 7)
    for i, (s, t) in enumerate(order):
        block((s, s, t), old, order[i + 1] if i < 7 else None)
        if i == 0:
            send_t(7, plane[7])
        elif i % 2 == 0:
            send_s(order[i - 1][0])
        old = (s, s, t)
    send_t(2, plane[2])
    to_t(1, 4, 4)
    send_t(4, plane[4])
    to_s(1, 4, 4)
    send_s(4)
    cross(x0, 0, 8, 0)
    cross(x1, 0, 8, 1)
    fill(k0, x0)
    fill(k1, x1)
    to_s(0, 0, 8)
    to_s(1, 0, 8)

    loads[3].wait()
    res, dirn = residual[...], direction[...]
    total = acc[0] + acc[NS]
    for slot in (0, 1, 2, 14, 12, 7, 9, 11, 13, 4, 5, 6, 8, 3, 10):
        out_copy(slot).wait_recv()
        total = total + got[slot].astype(F32)
    image = total * FACTOR + dirn
    image_ref[...] = image

    def lanes(value):
        return jnp.sum(value, axis=1, keepdims=True)

    lane = lax.broadcasted_iota(jnp.int32, (64, 128), 1)
    table = jnp.where(lane == 0, lanes(res * res), 0.0)
    table = jnp.where(lane == 1, lanes(dirn * image), table)
    table = jnp.where(lane == 2, lanes(res * image), table)
    table = jnp.where(lane == 3, lanes(image * image), table)
    mine[...] = jnp.concatenate([table, jnp.zeros_like(table)], axis=0).T[0:8, :]

    def one_copy(s):
        return remote(mine, one.at[s], one_send.at[s], one_recv.at[s], ring[s])

    def two_copy(t):
        return remote(two.at[0], two.at[t], two_send.at[t], two_recv.at[t], plane[t])

    for s in range(1, NS):
        one_copy(s).start()
    value = mine[...]
    for s in range(1, NS):
        one_copy(s).wait_recv()
        value = value + one[s]
    two[0] = value
    for t in range(1, NG):
        two_copy(t).start()
    for t in range(1, NG):
        two_copy(t).wait_recv()
        value = value + two[t]

    square = jnp.concatenate([value, jnp.zeros((120, 128), F32)], axis=0).T
    norm_old, curv = square[0:64, 0:1], square[0:64, 1:2]
    mixed, norm_image = square[0:64, 2:3], square[0:64, 3:4]
    alpha = norm_old / curv
    fresh = jnp.maximum(norm_old - alpha * (2.0 * mixed - alpha * norm_image), 0.0)
    beta = fresh / norm_old
    alpha_ref[...] = jnp.broadcast_to(alpha, (64, 512))
    beta_ref[...] = jnp.broadcast_to(beta, (64, 512))

    for s in range(1, NS):
        s_copy(s).wait_send()
        one_copy(s).wait_send()
    for t in range(1, NT + 1):
        t_copy(t).wait_send()
    for slot in range(15):
        out_copy(slot).wait_send()
    for t in range(1, NG):
        two_copy(t).wait_send()


def local(coords, lengthscale, solution, residual, direction):
    probes, points = direction.shape
    feats = coords.shape[0]
    dma = pltpu.SemaphoreType.DMA
    big = jax.ShapeDtypeStruct((probes, points), F32)
    image, alpha, beta = pl.pallas_call(
        kernel,
        out_shape=(big, big, big),
        in_specs=[pl.BlockSpec(memory_space=pl.ANY)] * 4,
        out_specs=[pl.BlockSpec(memory_space=pltpu.VMEM)] * 3,
        scratch_shapes=[
            pltpu.VMEM((feats, points), F32),
            pltpu.VMEM((1, feats), F32),
            pltpu.VMEM((probes, points), F32),
            pltpu.VMEM((probes, points), F32),
            pltpu.VMEM((17, 80, 512), BF16),
            pltpu.VMEM((NS, 512, 128), BF16),
            pltpu.VMEM((NT + 1, 96, 512), BF16),
            pltpu.VMEM((NS + 1, 64, 512), BF16),
            pltpu.VMEM((17, 64, 512), F32),
            pltpu.VMEM((15, 64, 512), BF16),
            pltpu.VMEM((15, 64, 512), BF16),
            pltpu.VMEM((512, WIDTH), F32),
            pltpu.VMEM((512, WIDTH), F32),
            pltpu.VMEM((512, WIDTH), BF16),
            pltpu.VMEM((512, WIDTH), BF16),
            pltpu.VMEM((8, 128), F32),
            pltpu.VMEM((NS, 8, 128), F32),
            pltpu.VMEM((NG, 8, 128), F32),
            dma((4,)), dma((17,)), dma((17,)), dma((15,)), dma((15,)), dma((8,)), dma((8,)), dma((16,)), dma((16,)),
        ],
        compiler_params=pltpu.CompilerParams(
            collective_id=0, has_side_effects=True, vmem_limit_bytes=VMEM
        ),
    )(coords, lengthscale[None, :], residual, direction)
    new_residual = residual - alpha * image
    return solution + alpha * direction, new_residual, new_residual + beta * direction


def solution(mesh):
    spec = P(None, ("row", "col"))
    return jax.shard_map(
        local, mesh=mesh, in_specs=(spec, P(), spec, spec, spec), out_specs=(spec, spec, spec), check_vma=False
    )
```

```python
import math

import jax
import jax.numpy as jnp
from jax import lax
from jax.experimental import pallas as pl
from jax.experimental.pallas import tpu as pltpu
from jax.sharding import PartitionSpec as P

MESH = pl.DeviceIdType.MESH
F32 = jnp.float32
BF16 = jnp.bfloat16

NS = 8
NT = 8
NG = 16
HALF = 4
LN2 = math.log(2.0)
SCALE = 5.0 / LN2**2
SHIFT = 1.5 / LN2
CONST = 0.75 / LN2**2
FACTOR = LN2**2 / 3.0 * 2.0**SHIFT
WIDTH = 256
VMEM = 60 * 2**20


def entries(x, factor=None):
    w = -SHIFT - x * lax.rsqrt(x)
    value = (w * w + CONST) * jnp.exp2(w)
    return (value if factor is None else value * factor).astype(BF16)


def pieces(value):
    high = value.astype(BF16).astype(F32)
    mid = (value - high).astype(BF16).astype(F32)
    low = (value - high - mid).astype(BF16).astype(F32)
    return high, mid, low


def kernel(
    coords_hbm, scale_hbm, residual_hbm, direction_hbm, image_ref, alpha_ref, beta_ref,
    coords, scale, residual, direction,
    blk, left, right, dir_s, acc, out, got, x0, x1, k0, k1, mine, one, two,
    load, blk_send, blk_recv, out_send, out_recv, one_send, one_recv, two_send, two_recv,
):
    row, col = lax.axis_index("row"), lax.axis_index("col")
    core, y, z_lo = lax.rem(row, 2), lax.rem(lax.div(row, 2), 4), lax.div(row, 8)
    x, z_hi = lax.rem(col, 4), lax.div(col, 4)
    group = lax.rem(z_hi * 2 + z_lo + 2 * y, 4) * 4 + y
    member = core * 4 + x

    ring = {}
    for s in range(1, NS):
        m = lax.rem(member + s, NS)
        ring[s] = (row - core + lax.div(m, 4), z_hi * 4 + lax.rem(m, 4))

    def across(t):
        g = lax.rem(group + t, NG)
        to_y = lax.rem(g, 4)
        to_z = lax.rem(2 * to_y + lax.div(g, 4), 4)
        return (lax.rem(to_z, 2) * 8 + to_y * 2 + core, lax.div(to_z, 2) * 4 + x)

    plane = {t: across(t) for t in range(1, NG)}

    loads = [
        pltpu.make_async_copy(src, dst, load.at[i])
        for i, (src, dst) in enumerate(
            ((coords_hbm, coords), (scale_hbm, scale), (direction_hbm, direction), (residual_hbm, residual))
        )
    ]
    for copy in loads:
        copy.start()

    barrier = pltpu.get_barrier_semaphore()
    for s in range(1, NS):
        pl.semaphore_signal(barrier, inc=1, device_id=ring[s], device_id_type=MESH)
    for t in range(1, NG):
        pl.semaphore_signal(barrier, inc=1, device_id=plane[t], device_id_type=MESH)

    def remote(src, dst, send, recv, where):
        return pltpu.make_async_remote_copy(
            src_ref=src, dst_ref=dst, send_sem=send, recv_sem=recv, device_id=where, device_id_type=MESH
        )

    def s_copy(s):
        return remote(blk.at[0], blk.at[s], blk_send.at[s], blk_recv.at[s], ring[s])

    def t_copy(t, where=None):
        slot = NS + t
        return remote(blk.at[0], blk.at[slot], blk_send.at[slot], blk_recv.at[slot], where or ring[1])

    def out_copy(slot, where=None):
        return remote(out.at[slot], got.at[slot], out_send.at[slot], out_recv.at[slot], where or ring[1])

    for copy in loads[0:3]:
        copy.wait()
    eye = lax.broadcasted_iota(jnp.int32, (16, 16), 0) == lax.broadcasted_iota(jnp.int32, (16, 16), 1)
    column = jnp.sum(jnp.where(eye, jnp.broadcast_to(scale[...], (16, 16)), 0.0), axis=1, keepdims=True)
    blk[0, 0:16, :] = (coords[...] / column).astype(BF16)
    blk[0, 16:80, :] = direction[...].astype(BF16)
    blk[NS] = blk[0]

    def features(slot):
        wide = blk[slot, 0:16, :].astype(F32)
        high, mid, low = pieces(jnp.sum(wide * wide, axis=0, keepdims=True))
        rows = lax.broadcasted_iota(jnp.int32, (8, 512), 0)
        norm = jnp.where(rows == 0, high, jnp.where(rows == 1, mid, jnp.where(rows == 2, low, 0.0)))
        return wide, norm, jnp.where(rows < 3, 1.0, 0.0)

    def prepare_s(s):
        wide, norm, ones = features(s)
        one_set = jnp.concatenate([wide, norm, ones], axis=0)
        four = jnp.concatenate([one_set, one_set, one_set, jnp.zeros_like(one_set)], axis=0)
        left[s] = four.T.astype(BF16)
        dir_s[s] = blk[s, 16:80, :]

    def prepare_t(t):
        wide, norm, ones = features(NS + t)
        turned = jnp.concatenate([wide * (-2.0 * SCALE), ones * SCALE, norm * SCALE], axis=0)
        high, mid, low = pieces(turned)
        right[t, 0:32, :] = high.astype(BF16)
        right[t, 32:64, :] = mid.astype(BF16)
        right[t, 64:96, :] = low.astype(BF16)

    def cross(x, s, t, half):
        for j in range(0, 512, WIDTH):
            dist = lax.dot_general(
                left[s, j : j + WIDTH, 0:96], right[t, :, half * WIDTH : (half + 1) * WIDTH],
                (((1,), (0,)), ((), ())), preferred_element_type=F32,
            )
            x[j : j + WIDTH, :] = jnp.maximum(dist, 1e-12)

    def fill(k, x, factor=None):
        for j in range(0, 512, WIDTH):
            k[j : j + WIDTH, :] = entries(x[j : j + WIDTH, :], factor)

    def to_t(half, s, t):
        acc[NS + t, :, half * WIDTH : (half + 1) * WIDTH] += lax.dot_general(
            dir_s[s], (k0, k1)[half][...], (((1,), (0,)), ((), ())), preferred_element_type=F32
        )

    def side_s(half, t):
        return lax.dot_general(
            blk[NS + t, 16:80, half * WIDTH : (half + 1) * WIDTH], (k0, k1)[half][...],
            (((1,), (1,)), ((), ())), preferred_element_type=F32,
        )

    def to_s(half, s, t):
        acc[s] += side_s(half, t)

    acc[...] = jnp.zeros_like(acc)
    k1[...] = jnp.zeros_like(k1)
    dir_s[NS] = jnp.zeros_like(dir_s[NS])
    prepare_s(0)
    prepare_t(0)

    pl.semaphore_wait(barrier, NS - 1 + NG - 1)
    for s in (4, 1, 3):
        s_copy(s).start()
    for t in (4, 2):
        t_copy(t, plane[NG - t]).start()
    s_copy(2).start()
    for t in (7, 5, 3, 1, 6, 8):
        t_copy(t, plane[NG - t]).start()


    def plan(q):
        late = q > 8
        t = lax.rem(jnp.where(late, 2 * q + 1, 5 * q + 5), 7) + 1
        t = jnp.where(q == 8, 8, t)
        base = jnp.where(q == 8, 1, jnp.where(late, HALF, 0))
        slots = [base, base + 1, base + 2, base + 3]
        return t, slots, slots[0:3] + [jnp.where(q == 8, NS, base + 3)]

    def block(now, old, following):
        (s, dir_of, t), (old_s, old_dir, old_t) = now, old
        to_t(1, old_dir, old_t)
        cross(x1, s, t, 1)
        to_s(1, old_s, old_t)
        fill(k0, x0)
        to_t(0, dir_of, t)
        if following is not None:
            cross(x0, following[0], following[1], 0)
        to_s(0, s, t)
        fill(k1, x1)

    def strip(q, carry):
        t, slots, dirs = plan(q)
        before_t, before_slots, before_dirs = plan(q - 1)
        before_t = jnp.where(q == 1, 0, before_t)
        before_slots = before_slots[0:3] + [jnp.where(q == 1, 2, before_slots[3])]
        before_dirs = before_dirs[0:3] + [jnp.where(q == 1, 2, before_dirs[3])]
        after_t, after_slots, _ = plan(q + 1)
        after_slots = [jnp.where(q == 13, 5, after_slots[0])]

        @pl.when(q < 7)
        def _():
            t_copy(after_t).wait_recv()
            prepare_t(after_t)


        @pl.when(q == 1)
        def _():
            for s in (5, 7, 6):
                s_copy(s).start()


        @pl.when(q == 7)
        def _():
            t_copy(8).wait_recv()
            prepare_t(8)
            for s in range(HALF + 1, NS):
                s_copy(s).wait_recv()
                prepare_s(s)

        old = (before_slots[3], before_dirs[3], before_t)
        for i in range(4):
            following = (after_slots[0], after_t) if i == 3 else (slots[i + 1], t)
            block((slots[i], dirs[i], t), old, following)
            old = (slots[i], dirs[i], t)

        @pl.when(q == 9)
        def _():
            send_t(8, plane[8])
            for s in range(1, HALF):
                send_s(s)

        @pl.when(q > 9)
        def _():
            send_t(before_t, across(before_t))

        return carry

    def send_t(t, where):
        out[NS - 2 + t] = acc[NS + t].astype(BF16)
        out_copy(NS - 2 + t, where).start()

    def send_s(s):
        out[s - 1] = acc[s].astype(BF16)
        out_copy(s - 1, ring[NS - s]).start()

    old = (1, NS, 0)
    order = (4, 1, 3, 2)
    for i, s in enumerate(order):
        if i < 2:
            s_copy(s).wait_recv()
            prepare_s(s)
            cross(x0, s, 0, 0)
        if i == 0:
            following = None
        elif i < 3:
            s_copy(order[i + 1]).wait_recv()
            prepare_s(order[i + 1])
            following = (order[i + 1], 0)
        else:
            t_copy(4).wait_recv()
            prepare_t(4)
            following = (0, 4)
        now = (s, NS if s == HALF else s, 0)
        block(now, old, following)
        old = now
    lax.fori_loop(1, 14, strip, 0)
    order = [(s, t) for s in (5, 6, 7, 4) for t in (2, 4)]
    old = (7, 7, 7)
    for i, (s, t) in enumerate(order):
        block((s, s, t), old, order[i + 1] if i < 7 else None)
        if i == 0:
            send_t(7, plane[7])
        elif i % 2 == 0:
            send_s(order[i - 1][0])
        old = (s, s, t)
    send_t(2, plane[2])
    to_t(1, 4, 4)
    send_t(4, plane[4])
    to_s(1, 4, 4)
    send_s(4)
    cross(x0, 0, 8, 0)
    cross(x1, 0, 8, 1)
    fill(k0, x0)
    fill(k1, x1)
    cross(x0, 0, 0, 0)
    cross(x1, 0, 0, 1)
    to_s(0, 0, 8)
    to_s(1, 0, 8)
    fill(k0, x0, FACTOR)
    fill(k1, x1, FACTOR)
    own = side_s(0, 0) + side_s(1, 0)

    loads[3].wait()
    res, dirn = residual[...], direction[...]
    total = acc[0] + acc[NS] + own * (1.0 / FACTOR)
    for slot in (0, 1, 2, 14, 12, 7, 9, 11, 13, 4, 5, 6, 8, 3, 10):
        out_copy(slot).wait_recv()
        total = total + got[slot].astype(F32)
    image = total * FACTOR + dirn
    image_ref[...] = image

    def lanes(value):
        return jnp.sum(value, axis=1, keepdims=True)

    lane = lax.broadcasted_iota(jnp.int32, (64, 128), 1)
    table = jnp.where(lane == 0, lanes(res * res), 0.0)
    table = jnp.where(lane == 1, lanes(dirn * image), table)
    table = jnp.where(lane == 2, lanes(res * image), table)
    table = jnp.where(lane == 3, lanes(image * image), table)
    mine[...] = jnp.concatenate([table, jnp.zeros_like(table)], axis=0).T[0:8, :]

    def one_copy(s):
        return remote(mine, one.at[s], one_send.at[s], one_recv.at[s], ring[s])

    def two_copy(t):
        return remote(two.at[0], two.at[t], two_send.at[t], two_recv.at[t], plane[t])

    for s in range(1, NS):
        one_copy(s).start()
    for s in range(1, NS):
        s_copy(s).wait_send()
    for t in range(1, NT + 1):
        t_copy(t).wait_send()
    for slot in range(15):
        out_copy(slot).wait_send()
    value = mine[...]
    for s in range(1, NS):
        one_copy(s).wait_recv()
        value = value + one[s]
    two[0] = value
    for t in range(1, NG):
        two_copy(t).start()
    for s in range(1, NS):
        one_copy(s).wait_send()
    for t in range(1, NG):
        two_copy(t).wait_recv()
        value = value + two[t]

    square = jnp.concatenate([value, jnp.zeros((120, 128), F32)], axis=0).T
    norm_old, curv = square[0:64, 0:1], square[0:64, 1:2]
    mixed, norm_image = square[0:64, 2:3], square[0:64, 3:4]
    alpha = norm_old / curv
    fresh = jnp.maximum(norm_old - alpha * (2.0 * mixed - alpha * norm_image), 0.0)
    beta = fresh / norm_old
    alpha_ref[...] = jnp.broadcast_to(alpha, (64, 512))
    beta_ref[...] = jnp.broadcast_to(beta, (64, 512))

    for t in range(1, NG):
        two_copy(t).wait_send()


def local(coords, lengthscale, solution, residual, direction):
    probes, points = direction.shape
    feats = coords.shape[0]
    dma = pltpu.SemaphoreType.DMA
    big = jax.ShapeDtypeStruct((probes, points), F32)
    image, alpha, beta = pl.pallas_call(
        kernel,
        out_shape=(big, big, big),
        in_specs=[pl.BlockSpec(memory_space=pl.ANY)] * 4,
        out_specs=[pl.BlockSpec(memory_space=pltpu.VMEM)] * 3,
        scratch_shapes=[
            pltpu.VMEM((feats, points), F32),
            pltpu.VMEM((1, feats), F32),
            pltpu.VMEM((probes, points), F32),
            pltpu.VMEM((probes, points), F32),
            pltpu.VMEM((17, 80, 512), BF16),
            pltpu.VMEM((NS, 512, 128), BF16),
            pltpu.VMEM((NT + 1, 96, 512), BF16),
            pltpu.VMEM((NS + 1, 64, 512), BF16),
            pltpu.VMEM((17, 64, 512), F32),
            pltpu.VMEM((15, 64, 512), BF16),
            pltpu.VMEM((15, 64, 512), BF16),
            pltpu.VMEM((512, WIDTH), F32),
            pltpu.VMEM((512, WIDTH), F32),
            pltpu.VMEM((512, WIDTH), BF16),
            pltpu.VMEM((512, WIDTH), BF16),
            pltpu.VMEM((8, 128), F32),
            pltpu.VMEM((NS, 8, 128), F32),
            pltpu.VMEM((NG, 8, 128), F32),
            dma((4,)), dma((17,)), dma((17,)), dma((15,)), dma((15,)), dma((8,)), dma((8,)), dma((16,)), dma((16,)),
        ],
        compiler_params=pltpu.CompilerParams(
            collective_id=0, has_side_effects=True, vmem_limit_bytes=VMEM
        ),
    )(coords, lengthscale[None, :], residual, direction)
    new_residual = residual - alpha * image
    return solution + alpha * direction, new_residual, new_residual + beta * direction


def solution(mesh):
    spec = P(None, ("row", "col"))
    return jax.shard_map(
        local, mesh=mesh, in_specs=(spec, P(), spec, spec, spec), out_specs=(spec, spec, spec), check_vma=False
    )
```

```python
import math

import jax
import jax.numpy as jnp
from jax import lax
from jax.experimental import pallas as pl
from jax.experimental.pallas import tpu as pltpu
from jax.sharding import PartitionSpec as P

MESH = pl.DeviceIdType.MESH
F32 = jnp.float32
BF16 = jnp.bfloat16

NS = 8
NT = 8
NG = 16
HALF = 4
LN2 = math.log(2.0)
SCALE = 5.0 / LN2**2
SHIFT = 1.5 / LN2
CONST = 0.75 / LN2**2
FACTOR = LN2**2 / 3.0 * 2.0**SHIFT
WIDTH = 256
VMEM = 60 * 2**20


def entries(x, factor=None):
    w = -SHIFT - x * lax.rsqrt(x)
    value = (w * w + CONST) * jnp.exp2(w)
    return (value if factor is None else value * factor).astype(BF16)


def pieces(value):
    high = value.astype(BF16).astype(F32)
    mid = (value - high).astype(BF16).astype(F32)
    low = (value - high - mid).astype(BF16).astype(F32)
    return high, mid, low


def kernel(
    coords_hbm, scale_hbm, residual_hbm, direction_hbm, image_ref, alpha_ref, beta_ref,
    coords, scale, residual, direction,
    blk, left, right, dir_s, acc, out, got, x0, x1, k0, k1, mine, one, two,
    load, blk_send, blk_recv, out_send, out_recv, one_send, one_recv, two_send, two_recv,
):
    row, col = lax.axis_index("row"), lax.axis_index("col")
    core, y, z_lo = lax.rem(row, 2), lax.rem(lax.div(row, 2), 4), lax.div(row, 8)
    x, z_hi = lax.rem(col, 4), lax.div(col, 4)
    group = lax.rem(z_hi * 2 + z_lo + 2 * y, 4) * 4 + y
    member = core * 4 + x

    ring = {}
    for s in range(1, NS):
        m = lax.rem(member + s, NS)
        ring[s] = (row - core + lax.div(m, 4), z_hi * 4 + lax.rem(m, 4))

    def across(t):
        g = lax.rem(group + t, NG)
        to_y = lax.rem(g, 4)
        to_z = lax.rem(2 * to_y + lax.div(g, 4), 4)
        return (lax.rem(to_z, 2) * 8 + to_y * 2 + core, lax.div(to_z, 2) * 4 + x)

    plane = {t: across(t) for t in range(1, NG)}

    loads = [
        pltpu.make_async_copy(src, dst, load.at[i])
        for i, (src, dst) in enumerate(
            ((coords_hbm, coords), (scale_hbm, scale), (direction_hbm, direction), (residual_hbm, residual))
        )
    ]
    for copy in loads:
        copy.start()

    barrier = pltpu.get_barrier_semaphore()
    for s in range(1, NS):
        pl.semaphore_signal(barrier, inc=1, device_id=ring[s], device_id_type=MESH)
    for t in range(1, NG):
        pl.semaphore_signal(barrier, inc=1, device_id=plane[t], device_id_type=MESH)

    def remote(src, dst, send, recv, where):
        return pltpu.make_async_remote_copy(
            src_ref=src, dst_ref=dst, send_sem=send, recv_sem=recv, device_id=where, device_id_type=MESH
        )

    def s_copy(s):
        return remote(blk.at[0], blk.at[s], blk_send.at[s], blk_recv.at[s], ring[s])

    def t_copy(t, where=None):
        slot = NS + t
        return remote(blk.at[0], blk.at[slot], blk_send.at[slot], blk_recv.at[slot], where or ring[1])

    def out_copy(slot, where=None):
        return remote(out.at[slot], got.at[slot], out_send.at[slot], out_recv.at[slot], where or ring[1])

    for copy in loads[0:3]:
        copy.wait()
    eye = lax.broadcasted_iota(jnp.int32, (16, 16), 0) == lax.broadcasted_iota(jnp.int32, (16, 16), 1)
    column = jnp.sum(jnp.where(eye, jnp.broadcast_to(scale[...], (16, 16)), 0.0), axis=1, keepdims=True)
    blk[0, 0:16, :] = (coords[...] / column).astype(BF16)
    blk[0, 16:80, :] = direction[...].astype(BF16)
    pl.semaphore_wait(barrier, NS - 1 + NG - 1)
    for s in (4, 1, 3):
        s_copy(s).start()
    for t in (4, 2):
        t_copy(t, plane[NG - t]).start()
    s_copy(2).start()
    for t in (7, 5, 3, 1, 6, 8):
        t_copy(t, plane[NG - t]).start()
    for s in (5, 7, 6):
        s_copy(s).start()
    blk[NS] = blk[0]

    def features(slot):
        wide = blk[slot, 0:16, :].astype(F32)
        high, mid, low = pieces(jnp.sum(wide * wide, axis=0, keepdims=True))
        rows = lax.broadcasted_iota(jnp.int32, (8, 512), 0)
        norm = jnp.where(rows == 0, high, jnp.where(rows == 1, mid, jnp.where(rows == 2, low, 0.0)))
        return wide, norm, jnp.where(rows < 3, 1.0, 0.0)

    def prepare_s(s):
        wide, norm, ones = features(s)
        one_set = jnp.concatenate([wide, norm, ones], axis=0)
        four = jnp.concatenate([one_set, one_set, one_set, jnp.zeros_like(one_set)], axis=0)
        left[s] = four.T.astype(BF16)
        dir_s[s] = blk[s, 16:80, :]

    def prepare_t(t):
        wide, norm, ones = features(NS + t)
        turned = jnp.concatenate([wide * (-2.0 * SCALE), ones * SCALE, norm * SCALE], axis=0)
        high, mid, low = pieces(turned)
        right[t, 0:32, :] = high.astype(BF16)
        right[t, 32:64, :] = mid.astype(BF16)
        right[t, 64:96, :] = low.astype(BF16)

    def cross(x, s, t, half):
        for j in range(0, 512, WIDTH):
            dist = lax.dot_general(
                left[s, j : j + WIDTH, 0:96], right[t, :, half * WIDTH : (half + 1) * WIDTH],
                (((1,), (0,)), ((), ())), preferred_element_type=F32,
            )
            x[j : j + WIDTH, :] = jnp.maximum(dist, 1e-12)

    def fill(k, x, factor=None):
        for j in range(0, 512, WIDTH):
            k[j : j + WIDTH, :] = entries(x[j : j + WIDTH, :], factor)

    def to_t(half, s, t):
        acc[NS + t, :, half * WIDTH : (half + 1) * WIDTH] += lax.dot_general(
            dir_s[s], (k0, k1)[half][...], (((1,), (0,)), ((), ())), preferred_element_type=F32
        )

    def side_s(half, t):
        return lax.dot_general(
            blk[NS + t, 16:80, half * WIDTH : (half + 1) * WIDTH], (k0, k1)[half][...],
            (((1,), (1,)), ((), ())), preferred_element_type=F32,
        )

    def to_s(half, s, t):
        acc[s] += side_s(half, t)

    acc[...] = jnp.zeros_like(acc)
    k1[...] = jnp.zeros_like(k1)
    dir_s[NS] = jnp.zeros_like(dir_s[NS])
    prepare_s(0)
    prepare_t(0)

    def plan(q):
        late = q > 8
        t = lax.rem(jnp.where(late, 2 * q + 1, 5 * q + 5), 7) + 1
        t = jnp.where(q == 8, 8, t)
        base = jnp.where(q == 8, 1, jnp.where(late, HALF, 0))
        slots = [base, base + 1, base + 2, base + 3]
        return t, slots, slots[0:3] + [jnp.where(q == 8, NS, base + 3)]

    def block(now, old, following):
        (s, dir_of, t), (old_s, old_dir, old_t) = now, old
        to_t(1, old_dir, old_t)
        cross(x1, s, t, 1)
        to_s(1, old_s, old_t)
        fill(k0, x0)
        to_t(0, dir_of, t)
        if following is not None:
            cross(x0, following[0], following[1], 0)
        to_s(0, s, t)
        fill(k1, x1)

    def pair(p, carry):
        q = 2 * p + 1
        plans = [plan(q), plan(q + 1)]
        before_t, before_slots, before_dirs = plan(q - 1)
        before_t = jnp.where(q == 1, 0, before_t)
        after_t, after_slots, _ = plan(q + 2)

        @pl.when(q < 7)
        def _():
            for t in (plans[1][0], after_t):
                t_copy(t).wait_recv()
                prepare_t(t)

        @pl.when(q == 7)
        def _():
            t_copy(8).wait_recv()
            prepare_t(8)
            for s in range(HALF + 1, NS):
                s_copy(s).wait_recv()
                prepare_s(s)

        old = (
            jnp.where(q == 1, 2, before_slots[3]), jnp.where(q == 1, 2, before_dirs[3]), before_t,
        )
        steps = [(plans[i // 4][1][i % 4], plans[i // 4][2][i % 4], plans[i // 4][0]) for i in range(8)]
        for i, now in enumerate(steps):
            following = (steps[i + 1][0], steps[i + 1][2]) if i < 7 else (jnp.where(q == 13, 5, after_slots[0]), after_t)
            block(now, old, following)
            old = now

        @pl.when(q == 9)
        def _():
            send_t(8, plane[8])
            for s in range(1, HALF):
                send_s(s)

        @pl.when(q > 9)
        def _():
            send_t(before_t, across(before_t))

        @pl.when(q > 8)
        def _():
            send_t(plans[0][0], across(plans[0][0]))

        return carry

    def send_t(t, where):
        out[NS - 2 + t] = acc[NS + t].astype(BF16)
        out_copy(NS - 2 + t, where).start()

    def send_s(s):
        out[s - 1] = acc[s].astype(BF16)
        out_copy(s - 1, ring[NS - s]).start()

    old = (1, NS, 0)
    order = (4, 1, 3, 2)
    for i, s in enumerate(order):
        if i < 2:
            s_copy(s).wait_recv()
            prepare_s(s)
            cross(x0, s, 0, 0)
        if i == 0:
            following = None
        elif i < 3:
            s_copy(order[i + 1]).wait_recv()
            prepare_s(order[i + 1])
            following = (order[i + 1], 0)
        else:
            t_copy(4).wait_recv()
            prepare_t(4)
            following = (0, 4)
        now = (s, NS if s == HALF else s, 0)
        block(now, old, following)
        old = now
    lax.fori_loop(0, 7, pair, 0)
    order = (5, 6, 7, 4)
    old = (7, 7, 2)
    for i, s in enumerate(order):
        block((s, s, 4), old, (order[i + 1], 4) if i < 3 else None)
        if i == 0:
            send_t(2, plane[2])
        else:
            send_s(order[i - 1])
        old = (s, s, 4)
    to_t(1, 4, 4)
    send_t(4, plane[4])
    to_s(1, 4, 4)
    send_s(4)
    cross(x0, 0, 8, 0)
    cross(x1, 0, 8, 1)
    fill(k0, x0)
    fill(k1, x1)
    cross(x0, 0, 0, 0)
    cross(x1, 0, 0, 1)
    to_s(0, 0, 8)
    to_s(1, 0, 8)
    fill(k0, x0, FACTOR)
    fill(k1, x1, FACTOR)
    own = side_s(0, 0) + side_s(1, 0)

    loads[3].wait()
    res, dirn = residual[...], direction[...]
    total = acc[0] + acc[NS] + own * (1.0 / FACTOR)
    for slot in (0, 1, 2, 14, 12, 7, 9, 11, 13, 8, 4, 5, 6, 3, 10):
        out_copy(slot).wait_recv()
        total = total + got[slot].astype(F32)
    image = total * FACTOR + dirn
    image_ref[...] = image

    def lanes(value):
        return jnp.sum(value, axis=1, keepdims=True)

    lane = lax.broadcasted_iota(jnp.int32, (64, 128), 1)
    table = jnp.where(lane == 0, lanes(res * res), 0.0)
    table = jnp.where(lane == 1, lanes(dirn * image), table)
    table = jnp.where(lane == 2, lanes(res * image), table)
    table = jnp.where(lane == 3, lanes(image * image), table)
    mine[...] = jnp.concatenate([table, jnp.zeros_like(table)], axis=0).T[0:8, :]

    def one_copy(s):
        return remote(mine, one.at[s], one_send.at[s], one_recv.at[s], ring[s])

    def two_copy(t):
        return remote(two.at[0], two.at[t], two_send.at[t], two_recv.at[t], plane[t])

    for s in range(1, NS):
        one_copy(s).start()
    for s in range(1, NS):
        s_copy(s).wait_send()
    for t in range(1, NT + 1):
        t_copy(t).wait_send()
    for slot in range(15):
        out_copy(slot).wait_send()
    value = mine[...]
    for s in range(1, NS):
        one_copy(s).wait_recv()
        value = value + one[s]
    two[0] = value
    for t in range(1, NG):
        two_copy(t).start()
    for s in range(1, NS):
        one_copy(s).wait_send()
    for t in range(1, NG):
        two_copy(t).wait_recv()
        value = value + two[t]

    square = jnp.concatenate([value, jnp.zeros((120, 128), F32)], axis=0).T
    norm_old, curv = square[0:64, 0:1], square[0:64, 1:2]
    mixed, norm_image = square[0:64, 2:3], square[0:64, 3:4]
    alpha = norm_old / curv
    fresh = jnp.maximum(norm_old - alpha * (2.0 * mixed - alpha * norm_image), 0.0)
    beta = fresh / norm_old
    alpha_ref[...] = jnp.broadcast_to(alpha, (64, 512))
    beta_ref[...] = jnp.broadcast_to(beta, (64, 512))

    for t in range(1, NG):
        two_copy(t).wait_send()


def local(coords, lengthscale, solution, residual, direction):
    probes, points = direction.shape
    feats = coords.shape[0]
    dma = pltpu.SemaphoreType.DMA
    big = jax.ShapeDtypeStruct((probes, points), F32)
    image, alpha, beta = pl.pallas_call(
        kernel,
        out_shape=(big, big, big),
        in_specs=[pl.BlockSpec(memory_space=pl.ANY)] * 4,
        out_specs=[pl.BlockSpec(memory_space=pltpu.VMEM)] * 3,
        scratch_shapes=[
            pltpu.VMEM((feats, points), F32),
            pltpu.VMEM((1, feats), F32),
            pltpu.VMEM((probes, points), F32),
            pltpu.VMEM((probes, points), F32),
            pltpu.VMEM((17, 80, 512), BF16),
            pltpu.VMEM((NS, 512, 128), BF16),
            pltpu.VMEM((NT + 1, 96, 512), BF16),
            pltpu.VMEM((NS + 1, 64, 512), BF16),
            pltpu.VMEM((17, 64, 512), F32),
            pltpu.VMEM((15, 64, 512), BF16),
            pltpu.VMEM((15, 64, 512), BF16),
            pltpu.VMEM((512, WIDTH), F32),
            pltpu.VMEM((512, WIDTH), F32),
            pltpu.VMEM((512, WIDTH), BF16),
            pltpu.VMEM((512, WIDTH), BF16),
            pltpu.VMEM((8, 128), F32),
            pltpu.VMEM((NS, 8, 128), F32),
            pltpu.VMEM((NG, 8, 128), F32),
            dma((4,)), dma((17,)), dma((17,)), dma((15,)), dma((15,)), dma((8,)), dma((8,)), dma((16,)), dma((16,)),
        ],
        compiler_params=pltpu.CompilerParams(
            collective_id=0, has_side_effects=True, vmem_limit_bytes=VMEM
        ),
    )(coords, lengthscale[None, :], residual, direction)
    new_residual = residual - alpha * image
    return solution + alpha * direction, new_residual, new_residual + beta * direction


def solution(mesh):
    spec = P(None, ("row", "col"))
    return jax.shard_map(
        local, mesh=mesh, in_specs=(spec, P(), spec, spec, spec), out_specs=(spec, spec, spec), check_vma=False
    )
```
